256 devices in a mesh: grp: 4 (over x_hi, core), par: 64 (over z, x_lo, y).
Axes of the slice: x: 4 (x_hi: 2, x_lo: 2; x = x_hi * 2 + x_lo), y: 4, z: 8, core: 2. Of those that a mesh axis runs over, the one named last changes fastest.
Arguments:
- activations: bfloat16 [4096, 98304], P('par', 'grp'), may hold values from -6 to 6
- out_grads: bfloat16 [11008, 98304], P('par', 'grp'), may hold values from -6 to 6
- example_ids: int32 [4, 24576], P('grp'), may hold values from 0 to 31, never falling along the last dimension, each value on 1 to 1536 neighbouring positions
- train_flags: int32 [128], P('grp'), may hold values 0 or 1
- in_proj: bfloat16 [4096, 32], P('par'), may hold values from -0.09375 to 0.09375
- out_proj: bfloat16 [11008, 32], P('par'), may hold values from -0.0546875 to 0.0546875
Outputs:
- kernel: float32 [128, 128], P('grp')
The draws below stay inside these ranges and needn't reach their ends.
Inputs may be any that keep to these rules, and one draw needn't show every extreme that they name: `example_ids`: along each row ids never fall; each of the 32 examples has 1 to 1536 tokens, one exactly 1536.
All inputs are finite; a program needn't handle non-finite values. No bound on the sum of `train_flags` on one device may be relied on, other than what follows from the above.
Results may differ from the reference program's by a relative error of at most 0.0003.
Values sent between devices are 32-bit elements; how exact they have to be, the bound alone decides.
No kernel may reach another device: no remote copies, remote signals or barrier semaphores. Data moves between devices by JAX's collectives and lax.ppermute only.
A program may use at most 128 MiB of HBM per device.

```python
import math
import jax
import jax.numpy as jnp
import numpy as np
from jax import lax

D = 4096
FF = 11008
PROJ_IN = 32
PROJ_OUT = 32
TOK_GRP = 24576
EX_GRP = 32
MOST_TOK = 1536
TOKENS = 98304
EXAMPLES = 128
N_GRP = 4


def plant(drawn, own_key, low, top_value):
    index_at = [jax.random.randint(jax.random.fold_in(own_key, axis), (), 0, length) for axis, length in enumerate(drawn.shape)]
    main_axis = drawn.shape.index(max(drawn.shape))
    neighbour = index_at[:main_axis] + [(index_at[main_axis] + 1) % drawn.shape[main_axis]] + index_at[main_axis + 1:]
    return drawn.at[tuple(index_at)].set(low).at[tuple(neighbour)].set(top_value)


def block_scale(key, dims, shards, smallest, high):
    gain, own = 1.0, jax.random.fold_in(key, 6)
    for dim, shards_of in shards:
        heights = jnp.exp(jax.random.uniform(jax.random.fold_in(own, dim), (shards_of,), jnp.float32, smallest / len(shards), high / len(shards)))
        gain = gain * jnp.repeat(heights, dims[dim] // shards_of).reshape([-1 if axis == dim else 1 for axis in range(len(dims))])
    return gain


def split_up(number_of, total, bound, lean):
    portions = [(1 << 20) // math.isqrt(grade ** lean) + 1 for grade in range(2, number_of + 1)]
    surplus, counts = total - bound - (number_of - 1), [1] * (number_of - 1)
    while surplus > 0:
        free = [i for i in range(number_of - 1) if counts[i] < bound]
        whole, left = sum([portions[i] for i in free]), surplus
        for i in free:
            addition = min(bound - counts[i], max(1, left * portions[i] // whole), surplus)
            counts[i] = counts[i] + addition
            surplus = surplus - addition
    return np.array([bound] + counts)


def ragged(own_key, amount, total, limit, slope):
    if amount == 2:
        one = jax.random.randint(own_key, (), max(1, total - limit), min(limit, total - 1) + 1)
        return jnp.stack([one, total - one])
    lengths = jnp.asarray(split_up(amount, total, limit, slope), jnp.int32)
    pairs = (amount - 1) // 2
    donor, sink = lengths[1:1 + 2 * pairs:2], lengths[2:2 + 2 * pairs:2]
    room = jnp.minimum(donor - 1, limit - sink)
    passed = jax.random.randint(jax.random.fold_in(own_key, 1), (pairs,), 0, 1 << 20) % (room + 1)
    lengths = lengths.at[1:1 + 2 * pairs:2].set(donor - passed).at[2:2 + 2 * pairs:2].set(sink + passed)
    return lengths[jax.random.permutation(jax.random.fold_in(own_key, 2), amount)]


def bell_draw(stream_key, extent, scale, limit, split=(), kind=jnp.bfloat16):
    drawn = jax.random.normal(stream_key, extent, jnp.float32) * scale
    if len(split) > 0:
        drawn = block_scale(stream_key, extent, split, -0.22, 0.18) * drawn
    return jnp.clip(drawn, min=-limit, max=limit).astype(kind)


def setup_inputs(seed: int = 0) -> dict:
    seeds = jax.random.split(jax.random.key(seed), 7)
    return {
        "activations": bell_draw(seeds[0], (D, TOKENS), 1.0, 6.0, ((0, 64), (1, 4))),
        "out_grads": bell_draw(seeds[1], (FF, TOKENS), 1.0, 6.0, ((0, 64), (1, 4))),
        "example_ids": jax.vmap(lambda own: jnp.searchsorted(jnp.cumsum(ragged(own, EX_GRP, TOK_GRP, MOST_TOK, 1)), jnp.arange(TOK_GRP), side="right"))(jax.random.split(seeds[2], N_GRP)).reshape((N_GRP, TOK_GRP)).astype(jnp.int32),
        "train_flags": plant((jax.random.randint(seeds[3], (EXAMPLES,), 0, 2) < 1).astype(jnp.int32), jax.random.fold_in(seeds[3], 1), 0, 1),
        "in_proj": bell_draw(seeds[4], (D, PROJ_IN), D ** -0.5, 0.09375, ((0, 64),)),
        "out_proj": bell_draw(seeds[5], (FF, PROJ_OUT), FF ** -0.5, 0.0546875, ((0, 64),)),
    }


def block_features(left_part, right_part, group_ids):
    count = left_part.shape[1]
    width = 2048 if count % 2048 == 0 else count
    steps = count // width
    lefts = left_part.reshape(PROJ_IN, steps, width).transpose(1, 0, 2)
    rights = right_part.reshape(PROJ_OUT, steps, width).transpose(1, 0, 2)
    idents = group_ids.reshape(steps, width)
    labels = jnp.arange(EX_GRP, dtype=jnp.int32)

    def add_block(total, packed):
        left_block, right_block, id_block = packed
        onehot = (id_block[None, :] == labels[:, None]).astype(jnp.float32)
        spread = (left_block[:, None, :] * onehot[None, :, :]).reshape(PROJ_IN * EX_GRP, width)
        summed = lax.dot_general(spread, right_block, (((1,), (1,)), ((), ())), precision=lax.Precision.HIGHEST)
        return total + summed.reshape(PROJ_IN, EX_GRP, PROJ_OUT), None

    start = jnp.zeros((PROJ_IN, EX_GRP, PROJ_OUT), jnp.float32)
    total, unused = lax.scan(add_block, start, (lefts, rights, idents))
    return total.transpose(1, 0, 2).reshape(EX_GRP, PROJ_IN * PROJ_OUT)


def group_features(packed):
    left_part, right_part, group_ids = packed
    return block_features(left_part, right_part, group_ids)


def reference(activations, out_grads, example_ids, train_flags, in_proj, out_proj):
    left_proj = lax.dot_general(in_proj, activations, (((0,), (0,)), ((), ())), preferred_element_type=jnp.float32)
    right_proj = lax.dot_general(out_proj, out_grads, (((0,), (0,)), ((), ())), preferred_element_type=jnp.float32)
    left_proj = left_proj.reshape(PROJ_IN, N_GRP, TOK_GRP).transpose(1, 0, 2)
    right_proj = right_proj.reshape(PROJ_OUT, N_GRP, TOK_GRP).transpose(1, 0, 2)
    features = lax.map(group_features, (left_proj, right_proj, example_ids))
    features = features.reshape(N_GRP * EX_GRP, PROJ_IN * PROJ_OUT)
    flags = train_flags.astype(jnp.float32)
    factor = 1.0 / (PROJ_IN * (TOK_GRP // EX_GRP))
    row_side = features * (flags * factor)[:, None]
    col_side = features * (1.0 - flags)[:, None]
    return jnp.dot(row_side, col_side.T, precision=lax.Precision.HIGHEST)
```

```python
import functools
import jax
import jax.numpy as jnp
from jax import lax
from jax.experimental import pallas as pl
from jax.experimental.pallas import tpu as pltpu
from jax.sharding import PartitionSpec as P

ROWS = 32
TOK_GRP = 24576
EX_GRP = 32
Z, X, Y = 8, 2, 4
BLOCK = TOK_GRP // (Z * X * Y)
SIZE = {"z": Z, "x": X, "y": Y}


def parts_of(index):
    return {"z": index // (X * Y), "x": index // Y % X, "y": index % Y}


def index_of(parts):
    return (parts["z"] * X + parts["x"]) * Y + parts["y"]


def send(value, axis, change):
    pairs = []
    for source in range(Z * X * Y):
        parts = parts_of(source)
        parts[axis] = change(parts[axis]) % SIZE[axis]
        pairs.append((source, index_of(parts)))
    return lax.ppermute(value, "par", pairs)


def up(value, axis):
    return send(value, axis, lambda at: at + 1)


def down(value, axis):
    return send(value, axis, lambda at: at - 1)


def pick(chunks, at):
    return lax.dynamic_index_in_dim(chunks, at, 0, keepdims=False)


def ring_sum(chunks, axis, at):
    count = SIZE[axis]
    far = count // 2
    own = lambda steps: pick(chunks, (at + steps) % count)
    opposite = own(far)
    half = opposite.shape[0] // 2
    rising, falling = up(opposite[:half], axis), down(opposite[half:], axis)
    ahead, behind = own(far - 1), own(1 - far)
    ahead = jnp.concatenate([ahead[:half] + rising, ahead[half:]])
    behind = jnp.concatenate([behind[:half], behind[half:] + falling])
    for steps in range(far - 1, 0, -1):
        rising, falling = up(ahead, axis), down(behind, axis)
        if steps > 1:
            ahead, behind = own(steps - 1) + rising, own(1 - steps) + falling
    return own(0) + rising + falling


def left_kernel(weight_ref, input_ref, out_ref):
    out = lax.dot_general(
        weight_ref[...], input_ref[...], (((0,), (0,)), ((), ())), preferred_element_type=jnp.float32
    )
    for y in range(Y):
        for x in range(X):
            at = (y * X + x) * BLOCK
            out_ref[0, y, x] = out[:, at : at + BLOCK]


def right_kernel(weight_ref, input_ref, out_ref):
    out = lax.dot_general(
        weight_ref[...], input_ref[...], (((0,), (0,)), ((), ())), preferred_element_type=jnp.float32
    )
    for y in range(Y):
        for x in range(X):
            at = (y * X + x) * BLOCK
            out_ref[y, x, 0] = out[:, at : at + BLOCK]


def projected(kernel, weight, inputs, shape, spec):
    depth = inputs.shape[0]
    wide = TOK_GRP // Z
    return pl.pallas_call(
        kernel,
        grid=(Z,),
        in_specs=[
            pl.BlockSpec((depth, ROWS), lambda step: (0, 0)),
            pl.BlockSpec((depth, wide), lambda step: (0, step)),
        ],
        out_specs=spec,
        out_shape=jax.ShapeDtypeStruct(shape, jnp.float32),
        compiler_params=pltpu.CompilerParams(vmem_limit_bytes=32 * 1024 * 1024),
    )(weight, inputs)


def feature_kernel(left_ref, right_ref, ids_ref, out_ref):
    labels = lax.broadcasted_iota(jnp.int32, (EX_GRP, BLOCK), 0)
    member = (ids_ref[...] == labels).astype(jnp.float32).astype(jnp.bfloat16)
    right = right_ref[...]
    over = (((1,), (1,)), ((), ()))
    for part in range(8):
        rows = [left_ref[part * 4 + a : part * 4 + a + 1, :] * right for a in range(4)]
        product = jnp.concatenate(rows, axis=0)
        high = product.astype(jnp.bfloat16)
        low = (product - high.astype(jnp.float32)).astype(jnp.bfloat16)
        out_ref[part] = lax.dot_general(
            member, high, over, preferred_element_type=jnp.float32
        ) + lax.dot_general(member, low, over, preferred_element_type=jnp.float32)


def on_device(activations, out_grads, example_ids, train_flags, in_proj, out_proj):
    index = lax.axis_index("par")
    at = parts_of(index)
    group = lax.axis_index("grp")

    left = projected(
        left_kernel, in_proj, activations, (Z, Y, X, ROWS, BLOCK),
        pl.BlockSpec((1, Y, X, ROWS, BLOCK), lambda step: (step, 0, 0, 0, 0)),
    )
    right = projected(
        right_kernel, out_proj, out_grads, (Y, X, Z, ROWS, BLOCK),
        pl.BlockSpec((Y, X, 1, ROWS, BLOCK), lambda step: (0, 0, step, 0, 0)),
    )

    left = ring_sum(left, "z", at["z"])
    left = ring_sum(left, "y", at["y"])
    left = pick(left, at["x"]) + send(pick(left, 1 - at["x"]), "x", lambda i: 1 - i)

    right = ring_sum(right, "y", at["y"])
    right = pick(right, at["x"]) + send(pick(right, 1 - at["x"]), "x", lambda i: 1 - i)
    right = ring_sum(right, "z", at["z"])

    place = (at["z"] * Y + at["y"]) * X + at["x"]
    ids = lax.dynamic_slice(example_ids, (0, place * BLOCK), (1, BLOCK))
    features = pl.pallas_call(
        feature_kernel,
        out_shape=jax.ShapeDtypeStruct((8, EX_GRP, 128), jnp.float32),
    )(left, right, ids)

    first, second = (at["y"] ^ (at["y"] >> 1)) & 1, at["y"] >> 1
    features = features.reshape(2, 4, EX_GRP, 128)
    features = pick(features, first) + send(pick(features, 1 - first), "y", lambda i: i ^ 1)
    features = features.reshape(2, 2, EX_GRP, 128)
    features = pick(features, second) + send(pick(features, 1 - second), "y", lambda i: i ^ 3)
    features = pick(features, at["x"]) + send(pick(features, 1 - at["x"]), "x", lambda i: 1 - i)
    for bit in (1, 2, 4):
        features = features + send(features, "z", lambda i: i ^ bit)

    flags = train_flags.astype(jnp.float32)
    row_side = features * (flags * (1.0 / TOK_GRP))[:, None]
    cols = (features * (1.0 - flags)[:, None])[None]
    for bit in (1, 2):
        other = lax.ppermute(cols, "grp", [(i, i ^ bit) for i in range(4)])
        late = (group & bit) > 0
        cols = jnp.concatenate([jnp.where(late, other, cols), jnp.where(late, cols, other)])
    cols = cols.reshape(4 * EX_GRP, 128)
    kernel = lax.dot_general(
        row_side, cols, (((1,), (1,)), ((), ())), precision=lax.Precision.HIGHEST
    )
    kernel = kernel + send(kernel, "y", lambda i: i ^ 1)
    kernel = kernel + send(kernel, "y", lambda i: i ^ 3)
    kernel = kernel + send(kernel, "x", lambda i: 1 - i)
    return kernel


def solution(mesh):
    return jax.shard_map(
        on_device,
        mesh=mesh,
        in_specs=(
            P("par", "grp"),
            P("par", "grp"),
            P("grp", None),
            P("grp"),
            P("par", None),
            P("par", None),
        ),
        out_specs=P("grp", None),
        check_vma=False,
    )
```

```python
import jax
import jax.numpy as jnp
from jax import lax
from jax.experimental import pallas as pl
from jax.experimental.pallas import tpu as pltpu
from jax.sharding import PartitionSpec as P

ROWS = 32
TOK_GRP = 24576
EX_GRP = 32
Z, X, Y = 8, 2, 4
LEFT = ROWS // Y
RIGHT = ROWS // X
WIDE = TOK_GRP // Z
SUB = WIDE // Y
SIZE = {"z": Z, "x": X, "y": Y}
MIB = 1024 * 1024
SMEM = pl.BlockSpec(memory_space=pltpu.SMEM)
VMEM = pl.BlockSpec(memory_space=pltpu.VMEM)


def parts_of(index):
    return {"z": index // (X * Y), "x": index // Y % X, "y": index % Y}


def index_of(parts):
    return (parts["z"] * X + parts["x"]) * Y + parts["y"]


def send(value, axis, change):
    pairs = []
    for source in range(Z * X * Y):
        parts = parts_of(source)
        parts[axis] = change(parts[axis]) % SIZE[axis]
        pairs.append((source, index_of(parts)))
    return lax.ppermute(value, "par", pairs)


def both_ways(rising, falling, axis):
    return send(rising, axis, lambda at: at + 1), send(falling, axis, lambda at: at - 1)


def mixed(value, axis, bits):
    return send(value, axis, lambda at: at ^ bits)


def local(kernel, at, values, shapes, scratch=(), alias=None):
    lead = [jnp.stack(at)] if at else []
    return pl.pallas_call(
        kernel,
        in_specs=[SMEM] * len(lead) + [VMEM] * len(values),
        out_specs=[VMEM] * len(shapes),
        out_shape=[pltpu.VMEM(shape, jnp.float32) for shape in shapes],
        scratch_shapes=[pltpu.VMEM(shape, jnp.float32) for shape in scratch],
        input_output_aliases=alias or {},
        compiler_params=pltpu.CompilerParams(vmem_limit_bytes=2 * MIB),
    )(*lead, *[pltpu.with_memory_space_constraint(value, pltpu.VMEM) for value in values])


def projections(at_ref, weight_ref, input_ref, buffer, arrived):
    copies = []
    for step in range(Z):
        begin = pl.multiple_of(lax.rem(at_ref[0] + step, Z) * WIDE, WIDE)
        copies.append(
            pltpu.make_async_copy(
                input_ref.at[:, pl.ds(begin, WIDE)], buffer.at[step], arrived.at[step]
            )
        )
        copies[-1].start()
    for step in range(Z):
        copies[step].wait()
        yield lax.dot_general(
            weight_ref[...], buffer[step], (((0,), (0,)), ((), ())), preferred_element_type=jnp.float32
        )


def left_kernel(at_ref, weight_ref, input_ref, *refs):
    outs, rising_ref, falling_ref = refs[:7], refs[7], refs[8]
    buffer, arrived = refs[9:]
    for step, out in enumerate(projections(at_ref, weight_ref, input_ref, buffer, arrived)):
        if step == Z // 2:
            rising_ref[...] = out[: ROWS // 2]
            falling_ref[...] = out[ROWS // 2 :]
        else:
            outs[step - (step > Z // 2)][...] = out


def right_kernel(at_ref, weight_ref, input_ref, own_ref, next_ref, last_ref, rising_ref, falling_ref, *rest):
    buffer, arrived, held = rest
    y, x = at_ref[1], at_ref[2]
    for step, out in enumerate(projections(at_ref, weight_ref, input_ref, buffer, arrived)):
        for sub in range(Y):
            for half in range(X):
                held[sub, half] = out[half * RIGHT : (half + 1) * RIGHT, sub * SUB : (sub + 1) * SUB]
        for half in range(X):
            rows = lax.rem(x + half, X)
            own_ref[half, step] = held[y, rows]
            next_ref[half, step] = held[lax.rem(y + 1, Y), rows]
            last_ref[half, step] = held[lax.rem(y + 3, Y), rows]
            (rising_ref if half == 0 else falling_ref)[step] = held[lax.rem(y + 2, Y), rows]


def projected(kernel, at, weight, inputs, shapes, scratch):
    depth = inputs.shape[0]
    return pl.pallas_call(
        kernel,
        in_specs=[SMEM, VMEM, pl.BlockSpec(memory_space=pltpu.HBM)],
        out_specs=[VMEM] * len(shapes),
        out_shape=[pltpu.VMEM(shape, jnp.float32) for shape in shapes],
        scratch_shapes=[
            pltpu.VMEM((Z, depth, WIDE), jnp.bfloat16),
            pltpu.SemaphoreType.DMA((Z,)),
            *scratch,
        ],
        compiler_params=pltpu.CompilerParams(vmem_limit_bytes=20 * MIB),
    )(jnp.stack(at), weight, pltpu.with_memory_space_constraint(inputs, pltpu.HBM))


def half_add_kernel(ahead_ref, behind_ref, rising_ref, falling_ref, up_ref, down_ref):
    half = rising_ref.shape[0]
    up_ref[:half] = ahead_ref[:half] + rising_ref[...]
    down_ref[half:] = behind_ref[half:] + falling_ref[...]


def half_add(ahead, behind, rising, falling):
    return local(
        half_add_kernel, (), [ahead, behind, rising, falling], [ahead.shape] * 2, alias={0: 0, 1: 1}
    )


def pair_add_kernel(ahead_ref, behind_ref, rising_ref, falling_ref, up_ref, down_ref):
    up_ref[...] = ahead_ref[...] + rising_ref[...]
    down_ref[...] = behind_ref[...] + falling_ref[...]


def pair_add(ahead, behind, rising, falling):
    return local(
        pair_add_kernel, (), [ahead, behind, rising, falling], [ahead.shape] * 2, alias={0: 0, 1: 1}
    )


def ring(chunks, rising, falling, axis):
    far = SIZE[axis] // 2
    moved = both_ways(rising, falling, axis)
    for steps in range(far - 1, 0, -1):
        add = half_add if steps == far - 1 else pair_add
        moved = both_ways(*add(chunks[steps], chunks[SIZE[axis] - steps], *moved), axis)
    return moved


def left_half_kernel(at_ref, own_ref, rising_ref, falling_ref, keep_ref, give_ref, held):
    total = own_ref[...] + rising_ref[...] + falling_ref[...]
    held[0], held[1] = total[: ROWS // 2], total[ROWS // 2 :]
    keep_ref[...] = held[at_ref[0]]
    give_ref[...] = held[1 - at_ref[0]]


def left_quarter_kernel(at_ref, own_ref, moved_ref, keep_ref, give_ref, held):
    total = own_ref[...] + moved_ref[...]
    held[0], held[1] = total[:LEFT], total[LEFT:]
    keep_ref[...] = held[at_ref[0]]
    give_ref[...] = held[1 - at_ref[0]]


def add_kernel(own_ref, moved_ref, out_ref):
    out_ref[...] = own_ref[...] + moved_ref[...]


def right_half_kernel(own_ref, rising_ref, falling_ref, keep_ref, give_ref):
    keep_ref[...] = own_ref[0] + rising_ref[0] + falling_ref[0]
    give_ref[...] = own_ref[1] + rising_ref[1] + falling_ref[1]


def right_chunks_kernel(own_ref, moved_ref, *refs):
    outs, rising_ref, falling_ref = refs[:7], refs[7], refs[8]
    for step in range(Z):
        total = own_ref[step] + moved_ref[step]
        if step == Z // 2:
            rising_ref[...] = total[: RIGHT // 2]
            falling_ref[...] = total[RIGHT // 2 :]
        else:
            outs[step - (step > Z // 2)][...] = total


def three_kernel(own_ref, rising_ref, falling_ref, out_ref):
    out_ref[...] = own_ref[...] + rising_ref[...] + falling_ref[...]


def spread(outs):
    return [*outs[: Z // 2], None, *outs[Z // 2 : Z - 1]], outs[Z - 1], outs[Z]


def feature_kernel(at_ref, left_ref, moved_ref, first_ref, second_ref, pair_ref, ids_ref, out_ref, held):
    left = left_ref[...] + moved_ref[...]
    for sub in range(Y):
        held[sub] = left[:, sub * SUB : (sub + 1) * SUB]
    labels = lax.broadcasted_iota(jnp.int32, (EX_GRP, SUB), 0)
    over = (((1,), (1,)), ((), ()))
    total = jnp.zeros((EX_GRP, LEFT * RIGHT), jnp.float32)
    pieces = [first_ref[...], second_ref[...], pair_ref[0], pair_ref[1]]
    for bits, right in zip((0, 1, 3, 2), pieces):
        sub = at_ref[0] ^ bits
        member = (ids_ref[sub] == labels).astype(jnp.float32).astype(jnp.bfloat16)
        part = held[sub]
        product = jnp.concatenate([part[a : a + 1] * right for a in range(LEFT)], axis=0)
        high = product.astype(jnp.bfloat16)
        low = (product - high.astype(jnp.float32)).astype(jnp.bfloat16)
        total += lax.dot_general(member, high, over, preferred_element_type=jnp.float32)
        total += lax.dot_general(member, low, over, preferred_element_type=jnp.float32)
    out_ref[...] = total


def on_device(activations, out_grads, example_ids, train_flags, in_proj, out_proj):
    at = parts_of(lax.axis_index("par"))
    group = lax.axis_index("grp")
    place = (at["z"], at["y"], at["x"])

    quarter = (X, Z, RIGHT, SUB)
    own, ahead, behind, rising, falling = projected(
        right_kernel, place, out_proj, out_grads, [quarter] * 3 + [quarter[1:]] * 2,
        [pltpu.VMEM((Y, X, RIGHT, SUB), jnp.float32)],
    )
    moved = both_ways(rising, falling, "y")
    left, low, high = spread(
        projected(left_kernel, place, in_proj, activations, [(ROWS, WIDE)] * 7 + [(ROWS // 2, WIDE)] * 2, [])
    )

    rising, falling = ring(left, low, high, "z")
    first, second = (at["y"] ^ (at["y"] >> 1)) & 1, at["y"] >> 1
    keep, give = local(
        left_half_kernel, (first,), [left[0], rising, falling], [(ROWS // 2, WIDE)] * 2,
        [(2, ROWS // 2, WIDE)],
    )
    keep, give = local(
        left_quarter_kernel, (second,), [keep, mixed(give, "y", 1)], [(LEFT, WIDE)] * 2, [(2, LEFT, WIDE)]
    )
    (left,) = local(add_kernel, (), [keep, mixed(give, "y", 3)], [(LEFT, WIDE)])
    left_moved = mixed(left, "x", 1)

    ahead, behind = local(
        right_first_kernel, (), [ahead, behind, *moved], [quarter] * 2, alias={0: 0, 1: 1}
    )
    rising, falling = both_ways(ahead, behind, "y")
    keep, give = local(right_half_kernel, (), [own, rising, falling], [quarter[1:]] * 2)
    right, low, high = spread(
        local(
            right_chunks_kernel, (), [keep, mixed(give, "x", 1)],
            [(RIGHT, SUB)] * 7 + [(RIGHT // 2, SUB)] * 2,
        )
    )
    rising, falling = ring(right, low, high, "z")
    (right,) = local(three_kernel, (), [right[0], rising, falling], [(RIGHT, SUB)])
    near = mixed(right, "y", 1)
    pair = mixed(jnp.stack([right, near]), "y", 3)

    ids = lax.dynamic_slice(example_ids, (0, at["z"] * WIDE), (1, WIDE)).reshape(Y, 1, SUB)
    features = pl.pallas_call(
        feature_kernel,
        in_specs=[SMEM] + [VMEM] * 6,
        out_specs=VMEM,
        out_shape=jax.ShapeDtypeStruct((EX_GRP, LEFT * RIGHT), jnp.float32),
        scratch_shapes=[pltpu.VMEM((Y, LEFT, SUB), jnp.float32)],
        compiler_params=pltpu.CompilerParams(vmem_limit_bytes=8 * MIB),
    )(jnp.stack([at["y"]]), left, left_moved, right, near, pair, ids)
    for bits in (1, 2, 7):
        features = features + mixed(features, "z", bits)

    flags = train_flags.astype(jnp.float32)
    row_side = features * (flags * (1.0 / TOK_GRP))[:, None]
    cols = (features * (1.0 - flags)[:, None])[None]
    for bit in (1, 2):
        other = lax.ppermute(cols, "grp", [(i, i ^ bit) for i in range(4)])
        late = (group & bit) > 0
        cols = jnp.concatenate([jnp.where(late, other, cols), jnp.where(late, cols, other)])
    cols = cols.reshape(4 * EX_GRP, LEFT * RIGHT)
    kernel = lax.dot_general(
        row_side, cols, (((1,), (1,)), ((), ())), precision=lax.Precision.HIGHEST
    )
    kernel = kernel + mixed(kernel, "y", 1)
    kernel = kernel + mixed(kernel, "y", 3)
    return kernel + mixed(kernel, "x", 1)


def right_first_kernel(ahead_ref, behind_ref, rising_ref, falling_ref, up_ref, down_ref):
    up_ref[0] = ahead_ref[0] + rising_ref[...]
    down_ref[1] = behind_ref[1] + falling_ref[...]


def solution(mesh):
    return jax.shard_map(
        on_device,
        mesh=mesh,
        in_specs=(
            P("par", "grp"),
            P("par", "grp"),
            P("grp", None),
            P("grp"),
            P("par", None),
            P("par", None),
        ),
        out_specs=P("grp", None),
        check_vma=False,
    )
```

```python
import jax
import jax.numpy as jnp
from jax import lax
from jax.experimental import pallas as pl
from jax.experimental.pallas import tpu as pltpu
from jax.sharding import PartitionSpec as P

ROWS = 32
TOK_GRP = 24576
EX_GRP = 32
Z, X, Y = 8, 2, 4
LEFT = ROWS // Y
RIGHT = ROWS // X
WIDE = TOK_GRP // Z
SUB = WIDE // Y
FAR, REST, ALL = (4,), (3, 5, 2, 6, 1, 7, 0), tuple(range(Z))
SIZE = {"z": Z, "x": X, "y": Y}
MIB = 1024 * 1024
SMEM = pl.BlockSpec(memory_space=pltpu.SMEM)
VMEM = pl.BlockSpec(memory_space=pltpu.VMEM)
ANY = pl.BlockSpec(memory_space=pl.ANY)


def parts_of(index):
    return {"z": index // (X * Y), "x": index // Y % X, "y": index % Y}


def index_of(parts):
    return (parts["z"] * X + parts["x"]) * Y + parts["y"]


def send(value, axis, change):
    pairs = []
    for source in range(Z * X * Y):
        parts = parts_of(source)
        parts[axis] = change(parts[axis]) % SIZE[axis]
        pairs.append((source, index_of(parts)))
    return lax.ppermute(value, "par", pairs)


def both_ways(rising, falling, axis):
    return send(rising, axis, lambda at: at + 1), send(falling, axis, lambda at: at - 1)


def mixed(value, axis, bits):
    return send(value, axis, lambda at: at ^ bits)


def ordered(kernel, count, after):
    return lambda *refs: kernel(*refs[:count], *refs[count + len(after) :])


def local(kernel, at, values, shapes, scratch=(), alias=None, after=()):
    lead = [jnp.stack(at)] if at else []
    return pl.pallas_call(
        ordered(kernel, len(lead) + len(values), after),
        in_specs=[SMEM] * len(lead) + [VMEM] * len(values) + [ANY] * len(after),
        out_specs=[VMEM] * len(shapes),
        out_shape=[pltpu.VMEM(shape, jnp.float32) for shape in shapes],
        scratch_shapes=[pltpu.VMEM(shape, jnp.float32) for shape in scratch],
        input_output_aliases=alias or {},
        compiler_params=pltpu.CompilerParams(vmem_limit_bytes=2 * MIB),
    )(*lead, *[pltpu.with_memory_space_constraint(value, pltpu.VMEM) for value in values], *after)


def projections(weight_ref, input_ref, held, buffer, arrived, starts):
    weight = pltpu.make_async_copy(weight_ref, held, arrived.at[len(starts)])
    weight.start()
    copies = []
    for place, begin in enumerate(starts):
        tokens = pl.ds(pl.multiple_of(begin, WIDE), WIDE)
        copies.append(
            pltpu.make_async_copy(input_ref.at[:, tokens], buffer.at[place], arrived.at[place])
        )
        copies[-1].start()
    weight.wait()
    for copy, place in zip(copies, range(len(starts))):
        copy.wait()
        yield jnp.dot(held[...], buffer[place], preferred_element_type=jnp.float32)


def begins(at_ref, steps):
    return [lax.rem(at_ref[0] + step, Z) * WIDE for step in steps]


def left_far_kernel(at_ref, weight_ref, input_ref, rising_ref, falling_ref, *scratch):
    (out,) = projections(weight_ref, input_ref, *scratch, begins(at_ref, FAR))
    rising_ref[...] = out[: ROWS // 2]
    falling_ref[...] = out[ROWS // 2 :]


def left_kernel(at_ref, weight_ref, input_ref, *refs):
    outs = projections(weight_ref, input_ref, *refs[-3:], begins(at_ref, REST))
    for out_ref, out in zip(refs[: len(REST)], outs):
        out_ref[...] = out


def right_kernel(
    at_ref, weight_ref, input_ref, own_ref, next_ref, last_ref, rising_ref, falling_ref, turned, *scratch
):
    y = at_ref[1]
    outs = projections(weight_ref, input_ref, *scratch, begins(at_ref, ALL))
    for step, out in enumerate(outs):
        for sub in range(Y):
            turned[sub] = out[:, sub * SUB : (sub + 1) * SUB]
        own_ref[step] = turned[y]
        next_ref[step] = turned[lax.rem(y + 1, Y)]
        last_ref[step] = turned[lax.rem(y + 3, Y)]
        (rising_ref if step < Z // 2 else falling_ref)[step % (Z // 2)] = turned[lax.rem(y + 2, Y)]


def projected(kernel, at, weight, inputs, blocks, shapes, turned=(), after=()):
    depth = inputs.shape[0]
    distant = lambda value: pltpu.with_memory_space_constraint(value, pltpu.HBM)
    return pl.pallas_call(
        ordered(kernel, 3, after),
        in_specs=[SMEM, *[pl.BlockSpec(memory_space=pltpu.HBM)] * 2] + [ANY] * len(after),
        out_specs=[VMEM] * len(shapes),
        out_shape=[pltpu.VMEM(shape, jnp.float32) for shape in shapes],
        scratch_shapes=[
            *turned,
            pltpu.VMEM((ROWS, depth), jnp.bfloat16),
            pltpu.VMEM((blocks, depth, WIDE), jnp.bfloat16),
            pltpu.SemaphoreType.DMA((blocks + 1,)),
        ],
        compiler_params=pltpu.CompilerParams(vmem_limit_bytes=20 * MIB),
    )(jnp.stack(at), distant(weight.T), distant(inputs), *after)


def half_add_kernel(ahead_ref, behind_ref, rising_ref, falling_ref, up_ref, down_ref):
    half = rising_ref.shape[0]
    up_ref[:half] = ahead_ref[:half] + rising_ref[...]
    down_ref[half:] = behind_ref[half:] + falling_ref[...]


def pair_add_kernel(ahead_ref, behind_ref, rising_ref, falling_ref, up_ref, down_ref):
    up_ref[...] = ahead_ref[...] + rising_ref[...]
    down_ref[...] = behind_ref[...] + falling_ref[...]


def step_add(ahead, behind, moved, after, half=False):
    kernel = half_add_kernel if half else pair_add_kernel
    return local(
        kernel, (), [ahead, behind, *moved], [ahead.shape] * 2, alias={0: 0, 1: 1}, after=after
    )


def left_half_kernel(at_ref, own_ref, rising_ref, falling_ref, keep_ref, give_ref, held):
    total = own_ref[...] + rising_ref[...] + falling_ref[...]
    held[0], held[1] = total[: ROWS // 2], total[ROWS // 2 :]
    keep_ref[...] = held[at_ref[0]]
    give_ref[...] = held[1 - at_ref[0]]


def left_quarter_kernel(at_ref, own_ref, moved_ref, keep_ref, give_ref, held):
    total = own_ref[...] + moved_ref[...]
    held[0], held[1] = total[:LEFT], total[LEFT:]
    keep_ref[...] = held[at_ref[0]]
    give_ref[...] = held[1 - at_ref[0]]


def add_kernel(own_ref, moved_ref, out_ref):
    out_ref[...] = own_ref[...] + moved_ref[...]


def right_chunks_kernel(own_ref, rising_ref, falling_ref, *refs):
    for step in ALL:
        total = own_ref[step] + rising_ref[step] + falling_ref[step]
        if step == FAR[0]:
            refs[-2][...] = total[: ROWS // 2]
            refs[-1][...] = total[ROWS // 2 :]
        else:
            refs[REST.index(step)][...] = total


def right_half_kernel(at_ref, *refs):
    *terms, keep_ref, give_ref, held = refs
    total = terms[0][...]
    for term in terms[1:]:
        total += term[...]
    held[0], held[1] = total[:RIGHT], total[RIGHT:]
    keep_ref[...] = held[at_ref[0]]
    give_ref[...] = held[1 - at_ref[0]]


def feature_kernel(at_ref, left_ref, moved_ref, ids_ref, *refs):
    *pieces, out_ref, held = refs
    left = left_ref[...] + moved_ref[...]
    for sub in range(Y):
        held[sub] = left[:, sub * SUB : (sub + 1) * SUB]
    labels = lax.broadcasted_iota(jnp.int32, (EX_GRP, SUB), 0)
    over = (((1,), (1,)), ((), ()))
    total = jnp.zeros((EX_GRP, LEFT * RIGHT), jnp.float32)
    for bits, piece in enumerate(pieces):
        right = piece[...]
        sub = at_ref[0] ^ bits
        member = (ids_ref[sub] == labels).astype(jnp.float32).astype(jnp.bfloat16)
        part = held[sub]
        product = jnp.concatenate([part[a : a + 1] * right for a in range(LEFT)], axis=0)
        high = product.astype(jnp.bfloat16)
        low = (product - high.astype(jnp.float32)).astype(jnp.bfloat16)
        total += lax.dot_general(member, high, over, preferred_element_type=jnp.float32)
        total += lax.dot_general(member, low, over, preferred_element_type=jnp.float32)
    out_ref[...] = total


def on_device(activations, out_grads, example_ids, train_flags, in_proj, out_proj):
    at = parts_of(lax.axis_index("par"))
    group = lax.axis_index("grp")
    place = (at["z"], at["y"])

    whole, half = (ROWS, WIDE), (ROWS // 2, WIDE)
    quarter = (Z, ROWS, SUB)
    far = projected(left_far_kernel, place, in_proj, activations, 1, [half] * 2)
    left_moved = both_ways(*far, "z")
    *right, rising, falling = projected(
        right_kernel, place, out_proj, out_grads, Z, [quarter] * 3 + [(Z // 2, ROWS, SUB)] * 2,
        [pltpu.VMEM((Y, ROWS, SUB), jnp.float32)], far[:1],
    )
    right_moved = both_ways(rising, falling, "y")
    left = projected(
        left_kernel, place, in_proj, activations, len(REST), [whole] * 7, after=[rising]
    )

    sent = step_add(left[0], left[1], left_moved, [], half=True)
    left_moved = both_ways(*sent, "z")
    sent = step_add(right[1], right[2], right_moved, sent[:1], half=True)
    right_moved = both_ways(*sent, "y")
    sent = step_add(left[2], left[3], left_moved, sent[:1])
    left_moved = both_ways(*sent, "z")
    sent = step_add(left[4], left[5], left_moved, sent[:1])
    left_moved = both_ways(*sent, "z")
    *right, rising, falling = local(
        right_chunks_kernel, (), [right[0], *right_moved],
        [(ROWS, SUB)] * 7 + [(ROWS // 2, SUB)] * 2, after=sent[:1],
    )
    right_moved = both_ways(rising, falling, "z")
    sent = step_add(right[0], right[1], right_moved, [], half=True)
    right_moved = both_ways(*sent, "z")
    first, second = (at["y"] ^ (at["y"] >> 1)) & 1, at["y"] >> 1
    keep, give = local(
        left_half_kernel, (first,), [left[6], *left_moved], [half] * 2, [(2, *half)], after=sent[:1]
    )
    left_moved = mixed(give, "y", 1)
    sent = step_add(right[2], right[3], right_moved, [give])
    right_moved = both_ways(*sent, "z")
    keep, give = local(
        left_quarter_kernel, (second,), [keep, left_moved], [(LEFT, WIDE)] * 2, [(2, LEFT, WIDE)],
        after=sent[:1],
    )
    left_moved = mixed(give, "y", 3)
    sent = step_add(right[4], right[5], right_moved, [give])
    right_moved = both_ways(*sent, "z")
    (left,) = local(add_kernel, (), [keep, left_moved], [(LEFT, WIDE)], after=sent[:1])
    left_moved = mixed(left, "x", 1)
    keep, give = local(
        right_half_kernel, (at["x"],), [right[6], *right_moved], [(RIGHT, SUB)] * 2, [(2, RIGHT, SUB)],
        after=[left],
    )
    (right,) = local(add_kernel, (), [keep, mixed(give, "x", 1)], [(RIGHT, SUB)])
    pieces = [right] + [mixed(right, "y", bits) for bits in range(1, Y)]

    ids = lax.dynamic_slice(example_ids, (0, at["z"] * WIDE), (1, WIDE)).reshape(Y, 1, SUB)
    features = pl.pallas_call(
        feature_kernel,
        in_specs=[SMEM] + [VMEM] * 7,
        out_specs=VMEM,
        out_shape=jax.ShapeDtypeStruct((EX_GRP, LEFT * RIGHT), jnp.float32),
        scratch_shapes=[pltpu.VMEM((Y, LEFT, SUB), jnp.float32)],
        compiler_params=pltpu.CompilerParams(vmem_limit_bytes=8 * MIB),
    )(jnp.stack([at["y"]]), left, left_moved, ids, *pieces)
    for bits in (1, 2, 7):
        features = features + mixed(features, "z", bits)

    flags = train_flags.astype(jnp.float32)
    row_side = features * (flags * (1.0 / TOK_GRP))[:, None]
    cols = (features * (1.0 - flags)[:, None])[None]
    for bit in (1, 2):
        other = lax.ppermute(cols, "grp", [(i, i ^ bit) for i in range(4)])
        late = (group & bit) > 0
        cols = jnp.concatenate([jnp.where(late, other, cols), jnp.where(late, cols, other)])
    cols = cols.reshape(4 * EX_GRP, LEFT * RIGHT)
    kernel = lax.dot_general(
        row_side, cols, (((1,), (1,)), ((), ())), precision=lax.Precision.HIGHEST
    )
    near, opposite, last = (mixed(kernel, "y", bits) for bits in range(1, Y))
    kernel = (kernel + near) + (opposite + last)
    return kernel + mixed(kernel, "x", 1)


def solution(mesh):
    return jax.shard_map(
        on_device,
        mesh=mesh,
        in_specs=(
            P("par", "grp"),
            P("par", "grp"),
            P("grp", None),
            P("grp"),
            P("par", None),
            P("par", None),
        ),
        out_specs=P("grp", None),
        check_vma=False,
    )
```

```python
import jax
import jax.numpy as jnp
from jax import lax
from jax.experimental import pallas as pl
from jax.experimental.pallas import tpu as pltpu
from jax.sharding import PartitionSpec as P

ROWS = 32
TOK_GRP = 24576
EX_GRP = 32
Z, X, Y = 8, 2, 4
LEFT = ROWS // X
RIGHT = ROWS // Y
WIDE = TOK_GRP // Z
HALF = WIDE // 2
FAR, REST, ALL = (4,), (3, 5, 2, 6, 1, 7, 0), tuple(range(Z))
SIZE = {"z": Z, "x": X, "y": Y}
MIB = 1024 * 1024
SMEM = pl.BlockSpec(memory_space=pltpu.SMEM)
VMEM = pl.BlockSpec(memory_space=pltpu.VMEM)
ANY = pl.BlockSpec(memory_space=pl.ANY)


def parts_of(index):
    return {"z": index // (X * Y), "x": index // Y % X, "y": index % Y}


def index_of(parts):
    return (parts["z"] * X + parts["x"]) * Y + parts["y"]


def send(value, axis, change):
    pairs = []
    for source in range(Z * X * Y):
        parts = parts_of(source)
        parts[axis] = change(parts[axis]) % SIZE[axis]
        pairs.append((source, index_of(parts)))
    return lax.ppermute(value, "par", pairs)


def both_ways(rising, falling, axis):
    return send(rising, axis, lambda at: at + 1), send(falling, axis, lambda at: at - 1)


def mixed(value, axis, bits):
    return send(value, axis, lambda at: at ^ bits)


def ordered(kernel, count, after):
    return lambda *refs: kernel(*refs[:count], *refs[count + len(after) :])


def local(kernel, at, values, shapes, scratch=(), alias=None, after=()):
    lead = [jnp.stack(at)] if at else []
    return pl.pallas_call(
        ordered(kernel, len(lead) + len(values), after),
        in_specs=[SMEM] * len(lead) + [VMEM] * len(values) + [ANY] * len(after),
        out_specs=[VMEM] * len(shapes),
        out_shape=[pltpu.VMEM(shape, jnp.float32) for shape in shapes],
        scratch_shapes=[pltpu.VMEM(shape, jnp.float32) for shape in scratch],
        input_output_aliases=alias or {},
        compiler_params=pltpu.CompilerParams(vmem_limit_bytes=2 * MIB),
    )(*lead, *[pltpu.with_memory_space_constraint(value, pltpu.VMEM) for value in values], *after)


def projections(weight_ref, input_ref, held, buffer, arrived, starts):
    weight = pltpu.make_async_copy(weight_ref, held, arrived.at[len(starts)])
    weight.start()
    copies = []
    for place, begin in enumerate(starts):
        tokens = pl.ds(pl.multiple_of(begin, WIDE), WIDE)
        copies.append(
            pltpu.make_async_copy(input_ref.at[:, tokens], buffer.at[place], arrived.at[place])
        )
        copies[-1].start()
    weight.wait()
    for copy, place in zip(copies, range(len(starts))):
        copy.wait()
        yield jnp.dot(held[...], buffer[place], preferred_element_type=jnp.float32)


def begins(at_ref, steps):
    return [lax.rem(at_ref[0] + step, Z) * WIDE for step in steps]


def left_far_kernel(at_ref, weight_ref, input_ref, rising_ref, falling_ref, *scratch):
    (out,) = projections(weight_ref, input_ref, *scratch, begins(at_ref, FAR))
    rising_ref[...] = out[: ROWS // 2]
    falling_ref[...] = out[ROWS // 2 :]


def left_kernel(at_ref, weight_ref, input_ref, *refs):
    outs = projections(weight_ref, input_ref, *refs[-3:], begins(at_ref, REST))
    for out_ref, out in zip(refs[: len(REST)], outs):
        out_ref[...] = out


def right_kernel(
    at_ref, weight_ref, input_ref, own_ref, next_ref, last_ref, rising_ref, falling_ref, turned, *scratch
):
    y = at_ref[1]
    outs = projections(weight_ref, input_ref, *scratch, begins(at_ref, ALL))
    for step, out in enumerate(outs):
        for row in range(Y):
            for side in range(2):
                tokens = out[row * RIGHT : (row + 1) * RIGHT, side * HALF : (side + 1) * HALF]
                turned[row, side] = tokens
        own_ref[step] = turned[y]
        next_ref[step] = turned[lax.rem(y + 1, Y)]
        last_ref[step] = turned[lax.rem(y + 3, Y)]
        (rising_ref if step < Z // 2 else falling_ref)[step % (Z // 2)] = turned[lax.rem(y + 2, Y)]


def projected(kernel, at, weight, inputs, blocks, shapes, turned=(), after=()):
    depth = inputs.shape[0]
    distant = lambda value: pltpu.with_memory_space_constraint(value, pltpu.HBM)
    return pl.pallas_call(
        ordered(kernel, 3, after),
        in_specs=[SMEM, *[pl.BlockSpec(memory_space=pltpu.HBM)] * 2] + [ANY] * len(after),
        out_specs=[VMEM] * len(shapes),
        out_shape=[pltpu.VMEM(shape, jnp.float32) for shape in shapes],
        scratch_shapes=[
            *turned,
            pltpu.VMEM((ROWS, depth), jnp.bfloat16),
            pltpu.VMEM((blocks, depth, WIDE), jnp.bfloat16),
            pltpu.SemaphoreType.DMA((blocks + 1,)),
        ],
        compiler_params=pltpu.CompilerParams(vmem_limit_bytes=20 * MIB),
    )(jnp.stack(at), distant(weight.T), distant(inputs), *after)


def half_add_kernel(ahead_ref, behind_ref, rising_ref, falling_ref, up_ref, down_ref):
    half = rising_ref.shape[0]
    up_ref[:half] = ahead_ref[:half] + rising_ref[...]
    down_ref[half:] = behind_ref[half:] + falling_ref[...]


def pair_add_kernel(ahead_ref, behind_ref, rising_ref, falling_ref, up_ref, down_ref):
    up_ref[...] = ahead_ref[...] + rising_ref[...]
    down_ref[...] = behind_ref[...] + falling_ref[...]


def step_add(ahead, behind, moved, after, half=False):
    kernel = half_add_kernel if half else pair_add_kernel
    return local(
        kernel, (), [ahead, behind, *moved], [ahead.shape] * 2, alias={0: 0, 1: 1}, after=after
    )


def left_half_kernel(at_ref, own_ref, rising_ref, falling_ref, keep_ref, give_ref, held):
    total = own_ref[...] + rising_ref[...] + falling_ref[...]
    held[0], held[1] = total[:LEFT], total[LEFT:]
    keep_ref[...] = held[at_ref[0]]
    give_ref[...] = held[1 - at_ref[0]]


def add_kernel(own_ref, moved_ref, out_ref):
    out_ref[...] = own_ref[...] + moved_ref[...]


def right_chunks_kernel(own_ref, rising_ref, falling_ref, *refs):
    for step in ALL:
        total = own_ref[step] + rising_ref[step] + falling_ref[step]
        if step == FAR[0]:
            refs[-2][...] = total[:1]
            refs[-1][...] = total[1:]
        else:
            refs[REST.index(step)][...] = total


def right_sum_kernel(own_ref, rising_ref, falling_ref, out_ref):
    out_ref[...] = own_ref[...] + rising_ref[...] + falling_ref[...]


def feature_kernel(own_ref, near_ref, opposite_ref, last_ref, right_ref, moved_ref, ids_ref, out_ref):
    left = (own_ref[...] + near_ref[...]) + (opposite_ref[...] + last_ref[...])
    labels = lax.broadcasted_iota(jnp.int32, (EX_GRP, HALF), 0)
    over = (((1,), (1,)), ((), ()))
    total = jnp.zeros((EX_GRP, LEFT * RIGHT), jnp.float32)
    for side in range(2):
        tokens = slice(side * HALF, (side + 1) * HALF)
        member = (ids_ref[:, tokens] == labels).astype(jnp.float32).astype(jnp.bfloat16)
        right = right_ref[side] + moved_ref[side]
        part = left[:, tokens]
        product = jnp.concatenate([part[a : a + 1] * right for a in range(LEFT)], axis=0)
        high = product.astype(jnp.bfloat16)
        low = (product - high.astype(jnp.float32)).astype(jnp.bfloat16)
        total += lax.dot_general(member, high, over, preferred_element_type=jnp.float32)
        total += lax.dot_general(member, low, over, preferred_element_type=jnp.float32)
    out_ref[...] = total


def on_device(activations, out_grads, example_ids, train_flags, in_proj, out_proj):
    at = parts_of(lax.axis_index("par"))
    group = lax.axis_index("grp")
    place = (at["z"], at["y"])

    whole, half = (ROWS, WIDE), (ROWS // 2, WIDE)
    chunk = (2, RIGHT, HALF)
    far = projected(left_far_kernel, place, in_proj, activations, 1, [half] * 2)
    left_moved = both_ways(*far, "z")
    *right, rising, falling = projected(
        right_kernel, place, out_proj, out_grads, Z, [(Z, *chunk)] * 3 + [(Z // 2, *chunk)] * 2,
        [pltpu.VMEM((Y, *chunk), jnp.float32)], far[:1],
    )
    right_moved = both_ways(rising, falling, "y")
    left = projected(
        left_kernel, place, in_proj, activations, len(REST), [whole] * 7, after=[rising]
    )

    sent = step_add(left[0], left[1], left_moved, [], half=True)
    left_moved = both_ways(*sent, "z")
    sent = step_add(right[1], right[2], right_moved, sent[:1], half=True)
    right_moved = both_ways(*sent, "y")
    sent = step_add(left[2], left[3], left_moved, sent[:1])
    left_moved = both_ways(*sent, "z")
    sent = step_add(left[4], left[5], left_moved, sent[:1])
    left_moved = both_ways(*sent, "z")
    *right, rising, falling = local(
        right_chunks_kernel, (), [right[0], *right_moved],
        [chunk] * 7 + [(1, RIGHT, HALF)] * 2, after=sent[:1],
    )
    right_moved = both_ways(rising, falling, "z")
    sent = step_add(right[0], right[1], right_moved, [], half=True)
    right_moved = both_ways(*sent, "z")
    keep, give = local(
        left_half_kernel, (at["x"],), [left[6], *left_moved], [half] * 2, [(2, *half)], after=sent[:1]
    )
    left_moved = mixed(give, "x", 1)
    sent = step_add(right[2], right[3], right_moved, [give])
    right_moved = both_ways(*sent, "z")
    (left,) = local(add_kernel, (), [keep, left_moved], [half], after=sent[:1])
    sent = step_add(right[4], right[5], right_moved, [])
    right_moved = both_ways(*sent, "z")
    lefts = [left] + [mixed(left, "y", bits) for bits in range(1, Y)]
    (right,) = local(right_sum_kernel, (), [right[6], *right_moved], [chunk])
    right_moved = mixed(right, "x", 1)

    ids = lax.dynamic_slice(example_ids, (0, at["z"] * WIDE), (1, WIDE))
    features = pl.pallas_call(
        feature_kernel,
        in_specs=[VMEM] * 7,
        out_specs=VMEM,
        out_shape=jax.ShapeDtypeStruct((EX_GRP, LEFT * RIGHT), jnp.float32),
        compiler_params=pltpu.CompilerParams(vmem_limit_bytes=12 * MIB),
    )(*lefts, right, right_moved, ids)
    for bits in (1, 2, 7):
        features = features + mixed(features, "z", bits)

    flags = train_flags.astype(jnp.float32)
    row_side = features * (flags * (1.0 / TOK_GRP))[:, None]
    cols = (features * (1.0 - flags)[:, None])[None]
    for bit in (1, 2):
        other = lax.ppermute(cols, "grp", [(i, i ^ bit) for i in range(4)])
        late = (group & bit) > 0
        cols = jnp.concatenate([jnp.where(late, other, cols), jnp.where(late, cols, other)])
    cols = cols.reshape(4 * EX_GRP, LEFT * RIGHT)
    kernel = lax.dot_general(
        row_side, cols, (((1,), (1,)), ((), ())), precision=lax.Precision.HIGHEST
    )
    near, opposite, last = (mixed(kernel, "y", bits) for bits in range(1, Y))
    kernel = (kernel + near) + (opposite + last)
    return kernel + mixed(kernel, "x", 1)


def solution(mesh):
    return jax.shard_map(
        on_device,
        mesh=mesh,
        in_specs=(
            P("par", "grp"),
            P("par", "grp"),
            P("grp", None),
            P("grp"),
            P("par", None),
            P("par", None),
        ),
        out_specs=P("grp", None),
        check_vma=False,
    )
```

```python
import jax
import jax.numpy as jnp
from jax import lax
from jax.experimental import pallas as pl
from jax.experimental.pallas import tpu as pltpu
from jax.sharding import PartitionSpec as P

ROWS = 32
TOK_GRP = 24576
EX_GRP = 32
Z, X, Y = 8, 2, 4
LEFT = ROWS // X
RIGHT = ROWS // Y
WIDE = TOK_GRP // Z
HALF = WIDE // 2
FAR, REST, ALL = (4,), (3, 5, 2, 6, 1, 7, 0), tuple(range(Z))
SIZE = {"z": Z, "x": X, "y": Y}
MIB = 1024 * 1024
SMEM = pl.BlockSpec(memory_space=pltpu.SMEM)
VMEM = pl.BlockSpec(memory_space=pltpu.VMEM)
ANY = pl.BlockSpec(memory_space=pl.ANY)


def parts_of(index):
    return {"z": index // (X * Y), "x": index // Y % X, "y": index % Y}


def index_of(parts):
    return (parts["z"] * X + parts["x"]) * Y + parts["y"]


def send(value, axis, change):
    pairs = []
    for source in range(Z * X * Y):
        parts = parts_of(source)
        parts[axis] = change(parts[axis]) % SIZE[axis]
        pairs.append((source, index_of(parts)))
    return lax.ppermute(value, "par", pairs)


def both_ways(rising, falling, axis):
    return send(rising, axis, lambda at: at + 1), send(falling, axis, lambda at: at - 1)


def mixed(value, axis, bits):
    return send(value, axis, lambda at: at ^ bits)


def ordered(kernel, count, after):
    return lambda *refs: kernel(*refs[:count], *refs[count + len(after) :])


def local(kernel, at, values, shapes, scratch=(), alias=None, after=()):
    lead = [jnp.stack(at)] if at else []
    return pl.pallas_call(
        ordered(kernel, len(lead) + len(values), after),
        in_specs=[SMEM] * len(lead) + [VMEM] * len(values) + [ANY] * len(after),
        out_specs=[VMEM] * len(shapes),
        out_shape=[pltpu.VMEM(shape, jnp.float32) for shape in shapes],
        scratch_shapes=[pltpu.VMEM(shape, jnp.float32) for shape in scratch],
        input_output_aliases=alias or {},
        compiler_params=pltpu.CompilerParams(vmem_limit_bytes=2 * MIB),
    )(*lead, *[pltpu.with_memory_space_constraint(value, pltpu.VMEM) for value in values], *after)


def projections(weight_ref, input_ref, held, buffer, arrived, starts):
    weight = pltpu.make_async_copy(weight_ref, held, arrived.at[len(starts)])
    weight.start()
    copies = []
    for place, begin in enumerate(starts):
        tokens = pl.ds(pl.multiple_of(begin, WIDE), WIDE)
        copies.append(
            pltpu.make_async_copy(input_ref.at[:, tokens], buffer.at[place], arrived.at[place])
        )
        copies[-1].start()
    weight.wait()
    for copy, place in zip(copies, range(len(starts))):
        copy.wait()
        yield jnp.dot(held[...], buffer[place], preferred_element_type=jnp.float32)


def begins(at_ref, steps):
    return [lax.rem(at_ref[0] + step, Z) * WIDE for step in steps]


def left_far_kernel(at_ref, weight_ref, input_ref, rising_ref, falling_ref, *scratch):
    (out,) = projections(weight_ref, input_ref, *scratch, begins(at_ref, FAR))
    rising_ref[...] = out[: ROWS // 2]
    falling_ref[...] = out[ROWS // 2 :]


def left_kernel(at_ref, weight_ref, input_ref, *refs):
    outs = projections(weight_ref, input_ref, *refs[-3:], begins(at_ref, REST))
    for out_ref, out in zip(refs[: len(REST)], outs):
        out_ref[...] = out


def right_kernel(
    at_ref, weight_ref, input_ref, own_ref, next_ref, last_ref, rising_ref, falling_ref, turned, *scratch
):
    y = at_ref[1]
    outs = projections(weight_ref, input_ref, *scratch, begins(at_ref, ALL))
    for step, out in enumerate(outs):
        for row in range(Y):
            for side in range(2):
                tokens = out[row * RIGHT : (row + 1) * RIGHT, side * HALF : (side + 1) * HALF]
                turned[row, side] = tokens
        own_ref[step] = turned[y]
        next_ref[step] = turned[lax.rem(y + 1, Y)]
        last_ref[step] = turned[lax.rem(y + 3, Y)]
        (rising_ref if step < Z // 2 else falling_ref)[step % (Z // 2)] = turned[lax.rem(y + 2, Y)]


def projected(kernel, at, weight, inputs, blocks, shapes, turned=(), after=()):
    depth = inputs.shape[0]
    distant = lambda value: pltpu.with_memory_space_constraint(value, pltpu.HBM)
    return pl.pallas_call(
        ordered(kernel, 3, after),
        in_specs=[SMEM, *[pl.BlockSpec(memory_space=pltpu.HBM)] * 2] + [ANY] * len(after),
        out_specs=[VMEM] * len(shapes),
        out_shape=[pltpu.VMEM(shape, jnp.float32) for shape in shapes],
        scratch_shapes=[
            *turned,
            pltpu.VMEM((ROWS, depth), jnp.bfloat16),
            pltpu.VMEM((blocks, depth, WIDE), jnp.bfloat16),
            pltpu.SemaphoreType.DMA((blocks + 1,)),
        ],
        compiler_params=pltpu.CompilerParams(vmem_limit_bytes=20 * MIB),
    )(jnp.stack(at), distant(weight.T), distant(inputs), *after)


def half_add_kernel(ahead_ref, behind_ref, rising_ref, falling_ref, up_ref, down_ref):
    half = rising_ref.shape[0]
    up_ref[:half] = ahead_ref[:half] + rising_ref[...]
    down_ref[half:] = behind_ref[half:] + falling_ref[...]


def pair_add_kernel(ahead_ref, behind_ref, rising_ref, falling_ref, up_ref, down_ref):
    up_ref[...] = ahead_ref[...] + rising_ref[...]
    down_ref[...] = behind_ref[...] + falling_ref[...]


def step_add(ahead, behind, moved, after, half=False):
    kernel = half_add_kernel if half else pair_add_kernel
    return local(
        kernel, (), [ahead, behind, *moved], [ahead.shape] * 2, alias={0: 0, 1: 1}, after=after
    )


def left_half_kernel(at_ref, own_ref, rising_ref, falling_ref, keep_ref, give_ref, held):
    total = own_ref[...] + rising_ref[...] + falling_ref[...]
    held[0], held[1] = total[:LEFT], total[LEFT:]
    keep_ref[...] = held[at_ref[0]]
    give_ref[...] = held[1 - at_ref[0]]


def add_kernel(own_ref, moved_ref, out_ref):
    out_ref[...] = own_ref[...] + moved_ref[...]


def right_chunks_kernel(own_ref, rising_ref, falling_ref, *refs):
    for step, out_ref in enumerate(refs):
        out_ref[...] = own_ref[step] + rising_ref[step] + falling_ref[step]


def right_sum_kernel(own_ref, rising_ref, falling_ref, out_ref):
    out_ref[...] = own_ref[...] + rising_ref[...] + falling_ref[...]


def feature_kernel(own_ref, other_ref, right_ref, moved_ref, ids_ref, out_ref):
    left = own_ref[...] + other_ref[...]
    labels = lax.broadcasted_iota(jnp.int32, (EX_GRP, HALF), 0)
    over = (((1,), (1,)), ((), ()))
    total = jnp.zeros((EX_GRP, LEFT * RIGHT), jnp.float32)
    for side in range(2):
        tokens = slice(side * HALF, (side + 1) * HALF)
        member = (ids_ref[:, tokens] == labels).astype(jnp.float32).astype(jnp.bfloat16)
        right = right_ref[side] + moved_ref[side]
        part = left[:, tokens]
        product = jnp.concatenate([part[a : a + 1] * right for a in range(LEFT)], axis=0)
        high = product.astype(jnp.bfloat16)
        low = (product - high.astype(jnp.float32)).astype(jnp.bfloat16)
        total += lax.dot_general(member, high, over, preferred_element_type=jnp.float32)
        total += lax.dot_general(member, low, over, preferred_element_type=jnp.float32)
    out_ref[...] = total


def on_device(activations, out_grads, example_ids, train_flags, in_proj, out_proj):
    at = parts_of(lax.axis_index("par"))
    group = lax.axis_index("grp")
    place = (at["z"], at["y"])

    whole, half = (ROWS, WIDE), (ROWS // 2, WIDE)
    chunk = (2, RIGHT, HALF)
    far = projected(left_far_kernel, place, in_proj, activations, 1, [half] * 2)
    left_moved = both_ways(*far, "z")
    *right, rising, falling = projected(
        right_kernel, place, out_proj, out_grads, Z, [(Z, *chunk)] * 3 + [(Z // 2, *chunk)] * 2,
        [pltpu.VMEM((Y, *chunk), jnp.float32)], far[:1],
    )
    right_moved = both_ways(rising, falling, "y")
    left = projected(
        left_kernel, place, in_proj, activations, len(REST), [whole] * 7, after=[rising]
    )

    sent = step_add(left[0], left[1], left_moved, [], half=True)
    left_moved = both_ways(*sent, "z")
    sent = step_add(right[1], right[2], right_moved, sent[:1], half=True)
    right_moved = both_ways(*sent, "y")
    sent = step_add(left[2], left[3], left_moved, sent[:1])
    left_moved = both_ways(*sent, "z")
    sent = step_add(left[4], left[5], left_moved, sent[:1])
    left_moved = both_ways(*sent, "z")
    right = local(right_chunks_kernel, (), [right[0], *right_moved], [chunk] * Z, after=sent[:1])
    right_moved = both_ways(right[4], right[5], "z")
    sent = step_add(right[3], right[6], right_moved, [])
    right_moved = both_ways(*sent, "z")
    keep, give = local(
        left_half_kernel, (at["x"],), [left[6], *left_moved], [half] * 2, [(2, *half)], after=sent[:1]
    )
    left_moved = mixed(give, "x", 1)
    sent = step_add(right[2], right[7], right_moved, [give])
    right_moved = both_ways(*sent, "z")
    (left,) = local(add_kernel, (), [keep, left_moved], [half], after=sent[:1])
    left_moved = mixed(left, "y", 1)
    (rising,) = local(add_kernel, (), [right[1], right_moved[0]], [chunk], after=[left])
    right_moved = [send(rising, "z", lambda at: at + 1), right_moved[1]]
    (left,) = local(add_kernel, (), [left, left_moved], [half], after=[rising])
    left_moved = mixed(left, "y", 3)
    (right,) = local(right_sum_kernel, (), [right[0], *right_moved], [chunk], after=[left])
    right_moved = mixed(right, "x", 1)

    ids = lax.dynamic_slice(example_ids, (0, at["z"] * WIDE), (1, WIDE))
    features = pl.pallas_call(
        feature_kernel,
        in_specs=[VMEM] * 5,
        out_specs=VMEM,
        out_shape=jax.ShapeDtypeStruct((EX_GRP, LEFT * RIGHT), jnp.float32),
        compiler_params=pltpu.CompilerParams(vmem_limit_bytes=12 * MIB),
    )(left, left_moved, right, right_moved, ids)
    for bits in (1, 2, 7):
        features = features + mixed(features, "z", bits)

    flags = train_flags.astype(jnp.float32)
    row_side = features * (flags * (1.0 / TOK_GRP))[:, None]
    cols = (features * (1.0 - flags)[:, None])[None]
    for bit in (1, 2):
        other = lax.ppermute(cols, "grp", [(i, i ^ bit) for i in range(4)])
        late = (group & bit) > 0
        cols = jnp.concatenate([jnp.where(late, other, cols), jnp.where(late, cols, other)])
    cols = cols.reshape(4 * EX_GRP, LEFT * RIGHT)
    kernel = lax.dot_general(
        row_side, cols, (((1,), (1,)), ((), ())), precision=lax.Precision.HIGHEST
    )
    near, opposite, last = (mixed(kernel, "y", bits) for bits in range(1, Y))
    kernel = (kernel + near) + (opposite + last)
    return kernel + mixed(kernel, "x", 1)


def solution(mesh):
    return jax.shard_map(
        on_device,
        mesh=mesh,
        in_specs=(
            P("par", "grp"),
            P("par", "grp"),
            P("grp", None),
            P("grp"),
            P("par", None),
            P("par", None),
        ),
        out_specs=P("grp", None),
        check_vma=False,
    )
```

```python
import jax
import jax.numpy as jnp
from jax import lax
from jax.experimental import pallas as pl
from jax.experimental.pallas import tpu as pltpu
from jax.sharding import PartitionSpec as P

ROWS = 32
TOK_GRP = 24576
EX_GRP = 32
Z, X, Y = 8, 2, 4
LEFT = ROWS // X
RIGHT = ROWS // Y
WIDE = TOK_GRP // Z
HALF = WIDE // 2
FAR, REST, ALL = (4, 5), (3, 6, 2, 7, 1, 0), tuple(range(Z))
SIZE = {"z": Z, "x": X, "y": Y}
MIB = 1024 * 1024
SMEM = pl.BlockSpec(memory_space=pltpu.SMEM)
VMEM = pl.BlockSpec(memory_space=pltpu.VMEM)
ANY = pl.BlockSpec(memory_space=pl.ANY)


def parts_of(index):
    return {"z": index // (X * Y), "x": index // Y % X, "y": index % Y}


def index_of(parts):
    return (parts["z"] * X + parts["x"]) * Y + parts["y"]


def send(value, axis, change):
    pairs = []
    for source in range(Z * X * Y):
        parts = parts_of(source)
        parts[axis] = change(parts[axis]) % SIZE[axis]
        pairs.append((source, index_of(parts)))
    return lax.ppermute(value, "par", pairs)


def both_ways(rising, falling, axis):
    return send(rising, axis, lambda at: at + 1), send(falling, axis, lambda at: at - 1)


def mixed(value, axis, bits):
    return send(value, axis, lambda at: at ^ bits)


def ordered(kernel, count, after):
    return lambda *refs: kernel(*refs[:count], *refs[count + len(after) :])


def local(kernel, at, values, shapes, scratch=(), alias=None, after=()):
    lead = [jnp.stack(at)] if at else []
    return pl.pallas_call(
        ordered(kernel, len(lead) + len(values), after),
        in_specs=[SMEM] * len(lead) + [VMEM] * len(values) + [ANY] * len(after),
        out_specs=[VMEM] * len(shapes),
        out_shape=[pltpu.VMEM(shape, jnp.float32) for shape in shapes],
        scratch_shapes=[pltpu.VMEM(shape, jnp.float32) for shape in scratch],
        input_output_aliases=alias or {},
        compiler_params=pltpu.CompilerParams(vmem_limit_bytes=2 * MIB),
    )(*lead, *[pltpu.with_memory_space_constraint(value, pltpu.VMEM) for value in values], *after)


def projections(weight_ref, input_ref, held, buffer, arrived, starts):
    weight = pltpu.make_async_copy(weight_ref, held, arrived.at[len(starts)])
    weight.start()
    copies = []
    for place, begin in enumerate(starts):
        tokens = pl.ds(pl.multiple_of(begin, WIDE), WIDE)
        copies.append(
            pltpu.make_async_copy(input_ref.at[:, tokens], buffer.at[place], arrived.at[place])
        )
        copies[-1].start()
    weight.wait()
    for copy, place in zip(copies, range(len(starts))):
        copy.wait()
        yield jnp.dot(held[...], buffer[place], preferred_element_type=jnp.float32)


def begins(at_ref, steps):
    return [lax.rem(at_ref[0] + step, Z) * WIDE for step in steps]


def left_far_kernel(at_ref, weight_ref, input_ref, *refs):
    outs = projections(weight_ref, input_ref, *refs[-3:], begins(at_ref, FAR))
    for out_ref, out in zip(refs[: len(FAR)], outs):
        out_ref[...] = out


def left_kernel(at_ref, weight_ref, input_ref, *refs):
    outs = projections(weight_ref, input_ref, *refs[-3:], begins(at_ref, REST))
    for out_ref, out in zip(refs[: len(REST)], outs):
        out_ref[...] = out


def right_kernel(
    at_ref, weight_ref, input_ref, own_ref, next_ref, last_ref, rising_ref, falling_ref, turned, *scratch
):
    y = at_ref[1]
    outs = projections(weight_ref, input_ref, *scratch, begins(at_ref, ALL))
    for step, out in enumerate(outs):
        for row in range(Y):
            for side in range(2):
                tokens = out[row * RIGHT : (row + 1) * RIGHT, side * HALF : (side + 1) * HALF]
                turned[row, side] = tokens
        own_ref[step] = turned[y]
        next_ref[step] = turned[lax.rem(y + 1, Y)]
        last_ref[step] = turned[lax.rem(y + 3, Y)]
        (rising_ref if step < Z // 2 else falling_ref)[step % (Z // 2)] = turned[lax.rem(y + 2, Y)]


def projected(kernel, at, weight, inputs, blocks, shapes, turned=(), after=()):
    depth = inputs.shape[0]
    distant = lambda value: pltpu.with_memory_space_constraint(value, pltpu.HBM)
    return pl.pallas_call(
        ordered(kernel, 3, after),
        in_specs=[SMEM, *[pl.BlockSpec(memory_space=pltpu.HBM)] * 2] + [ANY] * len(after),
        out_specs=[VMEM] * len(shapes),
        out_shape=[pltpu.VMEM(shape, jnp.float32) for shape in shapes],
        scratch_shapes=[
            *turned,
            pltpu.VMEM((ROWS, depth), jnp.bfloat16),
            pltpu.VMEM((blocks, depth, WIDE), jnp.bfloat16),
            pltpu.SemaphoreType.DMA((blocks + 1,)),
        ],
        compiler_params=pltpu.CompilerParams(vmem_limit_bytes=20 * MIB),
    )(jnp.stack(at), distant(weight.T), distant(inputs), *after)


def half_add_kernel(ahead_ref, behind_ref, rising_ref, falling_ref, up_ref, down_ref):
    half = rising_ref.shape[0]
    up_ref[:half] = ahead_ref[:half] + rising_ref[...]
    down_ref[half:] = behind_ref[half:] + falling_ref[...]


def pair_add_kernel(ahead_ref, behind_ref, rising_ref, falling_ref, up_ref, down_ref):
    up_ref[...] = ahead_ref[...] + rising_ref[...]
    down_ref[...] = behind_ref[...] + falling_ref[...]


def step_add(ahead, behind, moved, after, half=False):
    kernel = half_add_kernel if half else pair_add_kernel
    return local(
        kernel, (), [ahead, behind, *moved], [ahead.shape] * 2, alias={0: 0, 1: 1}, after=after
    )


def left_half_kernel(at_ref, own_ref, rising_ref, falling_ref, keep_ref, give_ref, held):
    total = own_ref[...] + rising_ref[...] + falling_ref[...]
    held[0], held[1] = total[:LEFT], total[LEFT:]
    keep_ref[...] = held[at_ref[0]]
    give_ref[...] = held[1 - at_ref[0]]


def add_kernel(own_ref, moved_ref, out_ref):
    out_ref[...] = own_ref[...] + moved_ref[...]


def right_chunks_kernel(own_ref, rising_ref, falling_ref, *refs):
    for step, out_ref in enumerate(refs):
        out_ref[...] = own_ref[step] + rising_ref[step] + falling_ref[step]


def right_sum_kernel(own_ref, rising_ref, falling_ref, out_ref):
    out_ref[...] = own_ref[...] + rising_ref[...] + falling_ref[...]


def feature_kernel(own_ref, other_ref, right_ref, moved_ref, ids_ref, out_ref):
    left = own_ref[...] + other_ref[...]
    labels = lax.broadcasted_iota(jnp.int32, (EX_GRP, HALF), 0)
    over = (((1,), (1,)), ((), ()))
    total = jnp.zeros((EX_GRP, LEFT * RIGHT), jnp.float32)
    for side in range(2):
        tokens = slice(side * HALF, (side + 1) * HALF)
        member = (ids_ref[:, tokens] == labels).astype(jnp.float32).astype(jnp.bfloat16)
        right = right_ref[side] + moved_ref[side]
        part = left[:, tokens]
        product = jnp.concatenate([part[a : a + 1] * right for a in range(LEFT)], axis=0)
        high = product.astype(jnp.bfloat16)
        low = (product - high.astype(jnp.float32)).astype(jnp.bfloat16)
        total += lax.dot_general(member, high, over, preferred_element_type=jnp.float32)
        total += lax.dot_general(member, low, over, preferred_element_type=jnp.float32)
    out_ref[...] = total


def on_device(activations, out_grads, example_ids, train_flags, in_proj, out_proj):
    at = parts_of(lax.axis_index("par"))
    group = lax.axis_index("grp")
    place = (at["z"], at["y"])

    whole, half = (ROWS, WIDE), (ROWS // 2, WIDE)
    chunk = (2, RIGHT, HALF)
    far = projected(left_far_kernel, place, in_proj, activations, len(FAR), [whole] * 2)
    left_moved = both_ways(*far, "z")
    *right, rising, falling = projected(
        right_kernel, place, out_proj, out_grads, Z, [(Z, *chunk)] * 3 + [(Z // 2, *chunk)] * 2,
        [pltpu.VMEM((Y, *chunk), jnp.float32)], far[:1],
    )
    right_moved = both_ways(rising, falling, "y")
    left = projected(
        left_kernel, place, in_proj, activations, len(REST), [whole] * 6, after=[rising]
    )

    sent = step_add(left[0], left[1], left_moved, [])
    left_moved = both_ways(*sent, "z")
    sent = step_add(right[1], right[2], right_moved, sent[:1], half=True)
    right_moved = both_ways(*sent, "y")
    sent = step_add(left[2], left[3], left_moved, sent[:1])
    left_moved = both_ways(*sent, "z")
    (rising,) = local(add_kernel, (), [left[4], left_moved[0]], [whole], after=sent[:1])
    left_moved = [send(rising, "z", lambda at: at + 1), left_moved[1]]
    right = local(right_chunks_kernel, (), [right[0], *right_moved], [chunk] * Z, after=[rising])
    right_moved = both_ways(right[4], right[5], "z")
    sent = step_add(right[3], right[6], right_moved, [])
    right_moved = both_ways(*sent, "z")
    keep, give = local(
        left_half_kernel, (at["x"],), [left[5], *left_moved], [half] * 2, [(2, *half)], after=sent[:1]
    )
    left_moved = mixed(give, "x", 1)
    sent = step_add(right[2], right[7], right_moved, [give])
    right_moved = both_ways(*sent, "z")
    (left,) = local(add_kernel, (), [keep, left_moved], [half], after=sent[:1])
    left_moved = mixed(left, "y", 1)
    (rising,) = local(add_kernel, (), [right[1], right_moved[0]], [chunk], after=[left])
    right_moved = [send(rising, "z", lambda at: at + 1), right_moved[1]]
    (left,) = local(add_kernel, (), [left, left_moved], [half], after=[rising])
    left_moved = mixed(left, "y", 3)
    (right,) = local(right_sum_kernel, (), [right[0], *right_moved], [chunk], after=[left])
    right_moved = mixed(right, "x", 1)

    ids = lax.dynamic_slice(example_ids, (0, at["z"] * WIDE), (1, WIDE))
    features = pl.pallas_call(
        feature_kernel,
        in_specs=[VMEM] * 5,
        out_specs=VMEM,
        out_shape=jax.ShapeDtypeStruct((EX_GRP, LEFT * RIGHT), jnp.float32),
        compiler_params=pltpu.CompilerParams(vmem_limit_bytes=12 * MIB),
    )(left, left_moved, right, right_moved, ids)
    for bits in (1, 2, 7):
        features = features + mixed(features, "z", bits)

    flags = train_flags.astype(jnp.float32)
    row_side = features * (flags * (1.0 / TOK_GRP))[:, None]
    cols = (features * (1.0 - flags)[:, None])[None]
    for bit in (1, 2):
        other = lax.ppermute(cols, "grp", [(i, i ^ bit) for i in range(4)])
        late = (group & bit) > 0
        cols = jnp.concatenate([jnp.where(late, other, cols), jnp.where(late, cols, other)])
    cols = cols.reshape(4 * EX_GRP, LEFT * RIGHT)
    kernel = lax.dot_general(
        row_side, cols, (((1,), (1,)), ((), ())), precision=lax.Precision.HIGHEST
    )
    near, opposite, last = (mixed(kernel, "y", bits) for bits in range(1, Y))
    kernel = (kernel + near) + (opposite + last)
    return kernel + mixed(kernel, "x", 1)


def solution(mesh):
    return jax.shard_map(
        on_device,
        mesh=mesh,
        in_specs=(
            P("par", "grp"),
            P("par", "grp"),
            P("grp", None),
            P("grp"),
            P("par", None),
            P("par", None),
        ),
        out_specs=P("grp", None),
        check_vma=False,
    )
```
